128 devices in a mesh: patch: 128 (over x, z, y, core).
Axes of the slice: x: 4, y: 4, z: 4, core: 2. Of those that a mesh axis runs over, the one named last changes fastest.
Arguments:
- noisy: float32 [1024, 4, 4, 1024], P('patch'), may hold values from -12 to 12
- sigma: float32 [4], replicated, may hold values from 0.5 to 4
- coarse: bfloat16 [12, 131072], P(None, 'patch'), may hold values from -6 to 6
- row_ids: int32 [1024, 16], P('patch'), may hold values from 0 to 131071, as said below
- table_index: int32 [1024], P('patch'), may hold values from 0 to 7
- interp_table: bfloat16 [8, 16, 1024], replicated, may hold values from -1.5 to 1.5
- live_counts: int32 [128], P('patch'), may hold values from 1 to 4
- face_len: int32 [1024, 2], P('patch'), may hold values from 1 to 32
- w_lift: bfloat16 [128, 16], replicated, may hold values from -1.5 to 1.5
- noise_embed: float32 [128], replicated, may hold values from -6 to 6
- kernel_top: bfloat16 [9, 128, 128], replicated, may hold values from -0.1875 to 0.1875
- w_down: bfloat16 [256, 128], replicated, may hold values from -0.5 to 0.5
- kernel_mid: bfloat16 [9, 256, 256], replicated, may hold values from -0.125 to 0.125
- w_up: bfloat16 [128, 256], replicated, may hold values from -0.375 to 0.375
- kernel_dec: bfloat16 [9, 128, 128], replicated, may hold values from -0.1875 to 0.1875
- w_out: bfloat16 [4, 128], replicated, may hold values from -0.5 to 0.5
Outputs:
- stepped: float32 [1024, 4, 4, 1024], P('patch')
The draws below stay inside these ranges and needn't reach their ends.
Inputs may be any that keep to these rules, and one draw needn't show every extreme that they name: `row_ids`: the coarse cells of patch p are local: each lies in [b * 1024 - 1024/2, (b + 1) * 1024 + 1024/2) with b = p // 8, the block of coarse cells held with the patch widened by half a block on each side.
All inputs are finite; a program needn't handle non-finite values.
Results may differ from the reference program's by a relative error of at most 0.00053.
Values may be sent and summed in bfloat16 or wider, within the bound.
A program may use at most 384 MiB of HBM per device.

```python
import math
import jax
import jax.numpy as jnp
from jax import lax

C = 128
C2 = 256
CC = 12
VARS = 4
H = 32
W = 32
RW = 16
NTAB = 8
ENS = 4
P_DEV = 8
CO_DEV = 1024
PATCHES = 1024
NCOARSE = 131072
N_PATCH = 128


def draw_row_ids(key, part):
    key = jax.random.fold_in(key, 11)
    key_main, key_low, key_high = jax.random.split(key, 3)
    half_block = CO_DEV // 2
    owners = jnp.arange(PATCHES, dtype=jnp.int32) // P_DEV
    offsets = jax.random.randint(key_main, (PATCHES, RW), -half_block, CO_DEV + half_block, dtype=jnp.int32)
    low_side = jax.random.randint(key_low, (PATCHES,), -half_block, 0, dtype=jnp.int32)
    high_side = jax.random.randint(key_high, (PATCHES,), CO_DEV, CO_DEV + half_block, dtype=jnp.int32)
    offsets = offsets.at[:, 0].set(low_side)
    offsets = offsets.at[:, 1].set(high_side)
    cells = owners[:, None] * CO_DEV + offsets
    return jnp.clip(cells, 0, NCOARSE - 1).astype(jnp.int32)


def touch_ends(array, stream_key, low, largest):
    dims = array.shape
    index_at = [jax.random.randint(jax.random.fold_in(stream_key, axis), (), 0, dims[axis]) for axis in range(len(dims))]
    array = array.at[tuple(index_at)].set(low)
    longest = dims.index(max(dims))
    index_at[longest] = (index_at[longest] + 1) % dims[longest]
    return array.at[tuple(index_at)].set(largest)


def block_scale(key, extent, shards, smallest, high):
    loudness = 1.0
    for position, blocks in shards:
        steps = jax.random.uniform(jax.random.fold_in(jax.random.fold_in(key, 6), position), (blocks,), jnp.float32, smallest / len(shards), high / len(shards))
        loudness = loudness * jnp.repeat(jnp.exp(steps), extent[position] // blocks).reshape((-1,) + (1,) * (len(extent) - 1 - position))
    return loudness


def noise(own_key, dims, scale, most, cuts=(), kind=jnp.bfloat16):
    drawn = scale * jax.random.normal(own_key, dims, jnp.float32)
    if cuts:
        drawn = drawn * block_scale(own_key, dims, cuts, -0.22, 0.18)
    return jnp.clip(drawn, -most, most).astype(kind)


def setup_inputs(seed: int = 0) -> dict:
    seeds = jax.random.split(jax.random.key(seed), 17)
    noisy = noise(seeds[0], (PATCHES, ENS, VARS, H * W), 2.0, 12.0, ((0, 128),), jnp.float32)
    sigma = jnp.clip(jnp.exp(jax.random.uniform(seeds[1], (ENS,), jnp.float32, math.log(0.5), math.log(4.0))), 0.5, 4.0)
    coarse = noise(seeds[2], (CC, NCOARSE), 1.0, 6.0, ((1, 128),))
    row_ids = draw_row_ids(jax.random.fold_in(seeds[16], 71), 0)
    table_index = touch_ends(jax.random.randint(seeds[4], (PATCHES,), 0, NTAB), jax.random.fold_in(seeds[4], 1), 0, NTAB - 1).astype(jnp.int32)
    interp_table = noise(seeds[5], (NTAB, RW, H * W), RW ** -0.5, 1.5)
    live_counts = touch_ends(jax.random.randint(seeds[6], (N_PATCH,), 1, (P_DEV + 1) // 2 + 1), jax.random.fold_in(seeds[6], 1), 1, ((P_DEV + 1) // 2 + 1) - 1).astype(jnp.int32)
    face_len = touch_ends(jax.random.randint(seeds[7], (PATCHES, 2), 1, W + 1), jax.random.fold_in(seeds[7], 1), 1, W).astype(jnp.int32)
    w_lift = noise(seeds[8], (C, VARS + CC), (VARS + CC) ** -0.5, 1.5)
    noise_embed = noise(seeds[9], (C,), 1.0, 6.0, (), jnp.float32)
    kernel_top = noise(seeds[10], (9, C, C), (9 * C) ** -0.5, 0.1875)
    w_down = noise(seeds[11], (C2, C), C ** -0.5, 0.5)
    kernel_mid = noise(seeds[12], (9, C2, C2), (9 * C2) ** -0.5, 0.125)
    w_up = noise(seeds[13], (C, C2), C2 ** -0.5, 0.375)
    kernel_dec = noise(seeds[14], (9, C, C), (9 * C) ** -0.5, 0.1875)
    w_out = noise(seeds[15], (VARS, C), C ** -0.5, 0.5)
    return dict(noisy=noisy, sigma=sigma, coarse=coarse, row_ids=row_ids, table_index=table_index, interp_table=interp_table, live_counts=live_counts, face_len=face_len, w_lift=w_lift, noise_embed=noise_embed, kernel_top=kernel_top, w_down=w_down, kernel_mid=kernel_mid, w_up=w_up, kernel_dec=kernel_dec, w_out=w_out)


SIGMA_DATA = 0.5
STEP_RATIO = 0.25
EPSILON = 1e-06

def rounded(value):
    return lax.optimization_barrier(value.astype(jnp.bfloat16)).astype(jnp.float32)

def normed(hidden):
    scale = lax.rsqrt(lax.optimization_barrier(jnp.mean(hidden * hidden, axis=2, keepdims=True)) + EPSILON)
    return lax.optimization_barrier(jax.nn.silu(hidden * scale).astype(jnp.bfloat16))

def bordered(act, alive, face_len, stride):
    row_width = act.shape[-1]
    keeper = alive.astype(jnp.bfloat16)[:, None, None, None]
    first_rows = act[:, :, :, 0, :] * keeper
    last_rows = act[:, :, :, -1, :] * keeper
    blank = jnp.zeros_like(first_rows[:1])
    above = jnp.concatenate([blank, last_rows[:-1]], axis=0)
    below = jnp.concatenate([first_rows[1:], blank], axis=0)
    columns = jnp.arange(row_width, dtype=jnp.int32) * stride
    mask_above = (columns[None, :] < face_len[:, 0:1]).astype(jnp.bfloat16)
    mask_below = (columns[None, :] < face_len[:, 1:2]).astype(jnp.bfloat16)
    above = above * mask_above[:, None, None, :]
    below = below * mask_below[:, None, None, :]
    full = jnp.concatenate([above[:, :, :, None, :], act, below[:, :, :, None, :]], axis=3)
    return jnp.pad(full, ((0, 0), (0, 0), (0, 0), (0, 0), (1, 1)))

def convolve(full, kernel):
    height = full.shape[3] - 2
    row_width = full.shape[4] - 2
    kern = kernel.astype(jnp.float32)

    def one_patch(block):
        values = block.astype(jnp.float32)
        total = jnp.zeros((values.shape[0], kernel.shape[1], height, row_width), jnp.float32)
        for tap_index in range(9):
            row_shift = tap_index // 3
            col_shift = tap_index % 3
            window = values[:, :, row_shift:row_shift + height, col_shift:col_shift + row_width]
            total = total + jnp.einsum('oc,echw->eohw', kern[tap_index], window)
        return total
    return lax.map(one_patch, full)

def reference(noisy, sigma, coarse, row_ids, table_index, interp_table, live_counts, face_len, w_lift, noise_embed, kernel_top, w_down, kernel_mid, w_up, kernel_dec, w_out):
    patches = noisy.shape[0]
    members = noisy.shape[1]
    slot_ids = jnp.arange(patches, dtype=jnp.int32)
    within = slot_ids % P_DEV
    alive = jnp.minimum(within, P_DEV - 1 - within) < live_counts[slot_ids // P_DEV]
    noise_sq = sigma * sigma + SIGMA_DATA * SIGMA_DATA
    c_in = lax.rsqrt(noise_sq)[None, :, None, None]
    c_skip = (SIGMA_DATA * SIGMA_DATA / noise_sq)[None, :, None, None]
    c_out = (sigma * SIGMA_DATA * lax.rsqrt(noise_sq))[None, :, None, None]
    picked = jnp.transpose(coarse[:, row_ids], (1, 0, 2)).astype(jnp.float32)
    stencils = interp_table[table_index].astype(jnp.float32)
    cond = jnp.einsum('pck,pkn->pcn', picked, stencils)
    cond_all = jnp.broadcast_to(cond[:, None], (patches, members, CC, H * W))
    lifted_in = rounded(jnp.concatenate([c_in * noisy, cond_all], axis=2))
    hidden = jnp.einsum('ck,pekn->pecn', w_lift.astype(jnp.float32), lifted_in)
    hidden = hidden + noise_embed[None, None, :, None] * jnp.log(sigma)[None, :, None, None]
    hidden = hidden.reshape(patches, members, C, H, W)
    top = hidden + convolve(bordered(normed(hidden), alive, face_len, 1), kernel_top)
    pooled = rounded(top.reshape(patches, members, C, H // 2, 2, W // 2, 2).mean(axis=(4, 6)))
    down = jnp.einsum('oc,pechw->peohw', w_down.astype(jnp.float32), pooled)
    middle = down + convolve(bordered(normed(down), alive, face_len, 2), kernel_mid)
    lifted = jnp.einsum('oc,pechw->peohw', w_up.astype(jnp.float32), rounded(middle))
    merged = top + jnp.repeat(jnp.repeat(lifted, 2, axis=3), 2, axis=4)
    decoded = merged + convolve(bordered(normed(merged), alive, face_len, 1), kernel_dec)
    network = jnp.einsum('vc,pechw->pevhw', w_out.astype(jnp.float32), normed(decoded).astype(jnp.float32))
    network = network.reshape(patches, members, VARS, H * W)
    denoised = c_skip * noisy + c_out * network
    moved = noisy + (STEP_RATIO - 1.0) * (noisy - denoised)
    return jnp.where(alive[:, None, None, None], moved, noisy)
```

```python
import functools

import jax
import jax.numpy as jnp
from jax import lax
from jax.experimental import pallas as pl
from jax.experimental.pallas import tpu as pltpu
from jax.sharding import PartitionSpec as P

MESH = pl.DeviceIdType.MESH
bf16 = jnp.bfloat16
f32 = jnp.float32

SLOTS = 8
ENS = 4
C = 128
C2 = 256
ROWS = 512
MROWS = 256
SIGMA_DATA = 0.5
STEP_RATIO = 0.25
EPSILON = 1e-06

NT = (((1,), (1,)), ((), ()))


def iota(shape, dim):
    return lax.broadcasted_iota(jnp.int32, shape, dim)


def half_silu(v, scale):
    h = v * scale
    return h + h * jnp.tanh(h)


def act_pair(v):
    halves = []
    for k in range(2):
        x = v[:, k * C : (k + 1) * C]
        scale = 0.5 * lax.rsqrt(jnp.mean(x * x, axis=1, keepdims=True) + EPSILON)
        halves.append(half_silu(x, scale))
    return halves


def act_wide(v):
    scale = 0.5 * lax.rsqrt(jnp.mean(v * v, axis=1, keepdims=True) + EPSILON)
    return half_silu(v, scale)


def from_left(x):
    n, c = x.shape
    x3 = x.reshape(n // 16, 16, c)
    return jnp.where(iota(x3.shape, 1) == 0, 0.0, pltpu.roll(x3, 1, 1)).reshape(n, c)


def from_right(x):
    n, c = x.shape
    x3 = x.reshape(n // 16, 16, c)
    return jnp.where(iota(x3.shape, 1) == 15, 0.0, pltpu.roll(x3, 15, 1)).reshape(n, c)


def transposed(block):
    return block.astype(f32).T.astype(bf16)


def kernel(
    noisy, sigma, coarse, row_ids, table_index, interp, live, face_len, w_lift, embed,
    k_top, w_down, k_mid, w_up, k_dec, w_out,
    out,
    cx, wtop, wdec, wmid, wup, wout, wlift, d_in,
    top, fc, fs, ha, hb, sha, shb, pool, mc, ml, mr, mha, mhb,
    rxa1, rxb1, rxa2, rxb2, rxa3, rxb3, send, recv,
):
    n = lax.axis_size("patch")
    me = lax.axis_index("patch")
    right, left = lax.rem(me + 1, n), lax.rem(me + n - 1, n)
    has_above = jnp.where(me > 0, 1.0, 0.0).astype(f32)
    has_below = jnp.where(me < n - 1, 1.0, 0.0).astype(f32)

    barrier = pltpu.get_barrier_semaphore()
    for neighbour in (left, right):
        pl.semaphore_signal(barrier, inc=1, device_id=(neighbour,), device_id_type=MESH)

    own = jnp.concatenate([coarse[...].astype(f32), jnp.zeros((4, 1024), f32)], axis=0)
    cx[:, 512:1536] = own.astype(bf16)

    pl.semaphore_wait(barrier, 2)

    def remote(src, dst, k, device):
        return pltpu.make_async_remote_copy(
            src_ref=src, dst_ref=dst, send_sem=send.at[k], recv_sem=recv.at[k],
            device_id=(device,), device_id_type=MESH,
        )

    cells_right = remote(cx.at[:, 1024:1536], cx.at[:, 0:512], 0, right)
    cells_left = remote(cx.at[:, 512:1024], cx.at[:, 1536:2048], 1, left)
    cells_right.start()
    cells_left.start()

    zero = jnp.zeros((C, C), bf16)
    for k_ref, w in ((k_top, wtop), (k_dec, wdec)):

        def fine_weights(dy, carry, k_ref=k_ref, w=w):
            taps = [transposed(k_ref[3 * dy + dx]) for dx in range(3)]
            rows = [(taps[1], taps[0]), (taps[2], taps[1]), (taps[0], zero), (zero, taps[2])]
            for i, (even, odd) in enumerate(rows):
                at = pl.multiple_of(dy * 512 + i * C, C)
                w[pl.ds(at, C), 0:C] = even
                w[pl.ds(at, C), C:C2] = odd
            return carry

        lax.fori_loop(0, 3, fine_weights, 0)

    def mid_weights(t, carry):
        wmid[pl.ds(pl.multiple_of(t * C2, C2), C2), :] = transposed(k_mid[t])
        return carry

    lax.fori_loop(0, 9, mid_weights, 0)
    wmid[2304:, :] = transposed(w_down[...])
    wup[...] = transposed(w_up[...])
    lane = iota((C, C), 0)
    for e in range(ENS):
        for par in range(2):
            z = jnp.zeros((C, C), f32)
            for v in range(4):
                row = w_out[v : v + 1, :].astype(f32)
                z = z + jnp.where(lane == par * 16 + e * 4 + v, row, 0.0)
            wout[e * C2 + par * C : e * C2 + (par + 1) * C, :] = z.T.astype(bf16)
        j = iota((C, 16), 0) % 32
        idx = iota((C, 16), 1)
        pick = ((j // 4 == e) & (idx == j % 4)) | ((j >= 16) & (j < 28) & (idx == j - 12))
        block = lax.dot_general(
            jnp.where(pick, 1.0, 0.0).astype(bf16), w_lift[...], NT, preferred_element_type=f32
        ).astype(bf16)
        wlift[e, 0:C, 0:C] = block
        wlift[e, 0:C, C:C2] = zero
        wlift[e, C:C2, 0:C] = zero
        wlift[e, C:C2, C:C2] = block

    def member(e, f):
        s = jnp.full((1, C), sigma[e], f32)
        return f(s)

    bias = []
    for e in range(ENS):
        b = embed[...] * member(e, jnp.log)
        bias.append(jnp.concatenate([b, b], axis=1))

    def per_row(f):
        r = iota((16, C), 0) // 4
        s = jnp.full((16, C), sigma[0], f32)
        for e in range(1, ENS):
            s = jnp.where(r == e, sigma[e], s)
        return f(s)[:, 0:1]

    c_in = per_row(lambda s: lax.rsqrt(s * s + SIGMA_DATA * SIGMA_DATA))
    c_skip = per_row(lambda s: SIGMA_DATA * SIGMA_DATA / (s * s + SIGMA_DATA * SIGMA_DATA))
    c_out = per_row(lambda s: s * SIGMA_DATA * lax.rsqrt(s * s + SIGMA_DATA * SIGMA_DATA))

    ids = row_ids[...] - (me * 1024 - 512)
    ids = jnp.concatenate([ids] * 8, axis=1)
    ids = jnp.where(iota((8, C), 1) // 16 == iota((8, C), 0), ids, 0)
    ids = jnp.sum(ids.astype(f32), axis=0, keepdims=True).astype(jnp.int32)
    one_hot = jnp.where(iota((2048, C), 0) == ids, 1.0, 0.0).astype(bf16)
    tab = jnp.zeros((C, C), jnp.int32)
    pk = iota((C, C), 0)
    tk = iota((C, C), 1)
    for p in range(SLOTS):
        tab = jnp.where(pk // 16 == p, table_index[p], tab)
    route = jnp.where((pk % 16 == tk % 16) & (tk // 16 == tab), 1.0, 0.0).astype(bf16)

    cells_right.wait()
    cells_left.wait()
    picked = jnp.dot(cx[...], one_hot, preferred_element_type=f32)
    picked = jnp.concatenate([picked] * 8, axis=0)
    picked = jnp.where(pk // 16 == tk // 16, picked, 0.0).astype(bf16)
    stencil = jnp.dot(picked, route, preferred_element_type=f32).astype(bf16)
    tables = interp[...].reshape(C, 1024)
    cond = jnp.dot(stencil, tables, preferred_element_type=f32).astype(bf16)
    for p in range(SLOTS):
        state = (noisy[p].reshape(16, 1024) * c_in).astype(bf16)
        for b in range(4):
            at = slice(b * C2, (b + 1) * C2)
            mr[b, p * 32 : p * 32 + 16, :] = state[:, at]
            mr[b, p * 32 + 16 : p * 32 + 32, :] = cond[p * 16 : p * 16 + 16, at]

    r = iota((C2, C2), 0)
    cell = iota((C2, C2), 1)
    split = jnp.where(cell == 2 * (r % C) + r // C, 1.0, 0.0).astype(bf16)
    for b in range(4):
        d = lax.dot_general(split, mr[b], NT, preferred_element_type=f32).astype(bf16)
        for t in range(2):
            for par in range(2):
                d_in[t, b * C : (b + 1) * C, par * C : (par + 1) * C] = d[
                    par * C : (par + 1) * C, t * C : (t + 1) * C
                ]

    fine_col = 2 * iota((16, C), 0)
    mid_col = 2 * iota((16, C2), 0)

    def alive(p):
        return jnp.where(jnp.minimum(p, SLOTS - 1 - p) < live[0], 1.0, 0.0).astype(f32)

    def face_of_next(p):
        return jnp.where(p == SLOTS - 1, 32, face_len[jnp.minimum(p + 1, SLOTS - 1), 0])

    def face_of_previous(p):
        return jnp.where(p == 0, 32, face_len[jnp.maximum(p - 1, 0), 1])

    def put_fine_face(centre, side, slot, e, even, odd, length, keep):
        even = jnp.where(fine_col < length, even, 0.0) * keep
        odd = jnp.where(fine_col + 1 < length, odd, 0.0) * keep
        centre[slot, e, :, 0:C] = even.astype(bf16)
        centre[slot, e, :, C:C2] = odd.astype(bf16)
        side[slot, e, :, 0:C] = from_left(odd).astype(bf16)
        side[slot, e, :, C:C2] = from_right(even).astype(bf16)

    def put_fine(p, e, even, odd):
        u = p * ENS + e
        fc[u, :, 0:C] = even.astype(bf16)
        fc[u, :, C:C2] = odd.astype(bf16)
        fs[u, :, 0:C] = from_left(odd).astype(bf16)
        fs[u, :, C:C2] = from_right(even).astype(bf16)
        keep = alive(p)
        put_fine_face(ha, sha, p + 1, e, even[ROWS - 16 :], odd[ROWS - 16 :], face_of_next(p), keep)
        put_fine_face(hb, shb, p, e, even[:16], odd[:16], face_of_previous(p), keep)

    def put_mid_face(faces, slot, e, a, length, keep):
        a = jnp.where(mid_col < length, a, 0.0) * keep
        faces[0, slot, e] = from_left(a).astype(bf16)
        faces[1, slot, e] = a.astype(bf16)
        faces[2, slot, e] = from_right(a).astype(bf16)

    def put_mid(p, e, a):
        u = p * ENS + e
        mc[u] = a.astype(bf16)
        ml[u] = from_left(a).astype(bf16)
        mr[u] = from_right(a).astype(bf16)
        keep = alive(p)
        put_mid_face(mha, p + 1, e, a[MROWS - 16 :], face_of_next(p), keep)
        put_mid_face(mhb, p, e, a[:16], face_of_previous(p), keep)

    def windows(ref, u, above, below, rows):
        return [
            jnp.concatenate([above, ref[u, 0 : rows - 16]], axis=0),
            ref[u],
            jnp.concatenate([ref[u, 16:rows], below], axis=0),
        ]

    def fine_conv(p, e, w):
        u = p * ENS + e
        centre = windows(fc, u, ha[p, e], hb[p + 1, e], ROWS)
        side = windows(fs, u, sha[p, e], shb[p + 1, e], ROWS)
        lhs = jnp.concatenate([x for pair in zip(centre, side) for x in pair], axis=1)
        return jnp.dot(lhs, w[...], preferred_element_type=f32)

    def mid_conv(p, e):
        u = p * ENS + e
        sides = [
            windows(ref, u, mha[k, p, e], mhb[k, p + 1, e], MROWS)
            for k, ref in enumerate((ml, mc, mr))
        ]
        taps = [sides[dx][dy] for dy in range(3) for dx in range(3)]
        lhs = jnp.concatenate(taps + [pool[u]], axis=1)
        return jnp.dot(lhs, wmid[...], preferred_element_type=f32)

    def fine_arrived(rxa, rxb):
        for e in range(ENS):
            a = rxa[e].astype(f32)
            put_fine_face(ha, sha, 0, e, a[:, :C], a[:, C:], face_len[0, 0], has_above)
            b = rxb[e].astype(f32)
            put_fine_face(hb, shb, SLOTS, e, b[:, :C], b[:, C:], face_len[SLOTS - 1, 1], has_below)

    def mid_arrived(rxa, rxb):
        for e in range(ENS):
            put_mid_face(mha, 0, e, rxa[e].astype(f32), face_len[0, 0], has_above)
            put_mid_face(mhb, SLOTS, e, rxb[e].astype(f32), face_len[SLOTS - 1, 1], has_below)

    def lift(i, carry):
        p = (i + 2) % SLOTS
        lanes = (iota((1, C2), 1) % C) // 32 == p % 4
        lhs = d_in[p // 4] * jnp.where(lanes, 1.0, 0.0).astype(bf16)
        for e in range(ENS):
            hidden = jnp.dot(lhs, wlift[e], preferred_element_type=f32) + bias[e]
            top[p * ENS + e] = hidden
            put_fine(p, e, *act_pair(hidden))
        return carry

    lax.fori_loop(0, SLOTS, lift, 0)
    face_down = remote(ha.at[SLOTS], rxa1, 2, right)
    face_up = remote(hb.at[0], rxb1, 3, left)
    face_down.start()
    face_up.start()

    def encode(i, carry):
        p = (i + 2) % SLOTS

        @pl.when(i == 5)
        def _():
            face_down.wait()
            face_up.wait()
            fine_arrived(rxa1, rxb1)

        for e in range(ENS):
            u = p * ENS + e
            t = top[u] + fine_conv(p, e, wtop)
            top[u] = t
            pooled = (t[:, :C] + t[:, C:]).reshape(16, 2, 16, C)
            pooled = ((pooled[:, 0] + pooled[:, 1]) * 0.25).reshape(MROWS, C).astype(bf16)
            pool[u] = pooled
            d = jnp.dot(pooled, wmid[2304:, :], preferred_element_type=f32)
            put_mid(p, e, act_wide(d))
        return carry

    lax.fori_loop(0, SLOTS, encode, 0)
    mid_down = remote(mha.at[1, SLOTS], rxa2, 4, right)
    mid_up = remote(mhb.at[1, 0], rxb2, 5, left)
    mid_down.start()
    mid_up.start()

    def middle(i, carry):
        p = (i + 2) % SLOTS

        @pl.when(i == 5)
        def _():
            mid_down.wait()
            mid_up.wait()
            mid_arrived(rxa2, rxb2)

        for e in range(ENS):
            u = p * ENS + e
            m = mid_conv(p, e).astype(bf16)
            up = jnp.dot(m, wup[...], preferred_element_type=f32).reshape(16, 1, 16, C)
            up = jnp.broadcast_to(up, (16, 2, 16, C)).reshape(ROWS, C)
            merged = top[u] + jnp.concatenate([up, up], axis=1)
            top[u] = merged
            put_fine(p, e, *act_pair(merged))
        return carry

    lax.fori_loop(0, SLOTS, middle, 0)
    last_down = remote(ha.at[SLOTS], rxa3, 6, right)
    last_up = remote(hb.at[0], rxb3, 7, left)
    last_down.start()
    last_up.start()

    cell_col = iota((C2, C2), 1)
    src = iota((C2, C2), 0)
    weave = jnp.where(cell_col == 2 * (src % C) + src // C, 1.0, 0.0).astype(bf16)

    def decode(i, carry):
        p = (i + 2) % SLOTS

        @pl.when(i == 5)
        def _():
            last_down.wait()
            last_up.wait()
            fine_arrived(rxa3, rxb3)

        for e in range(ENS):
            u = p * ENS + e
            even, odd = act_pair(top[u] + fine_conv(p, e, wdec))
            acts = jnp.concatenate([even, odd], axis=1).astype(bf16)
            mc[2 * e : 2 * e + 2] = acts.reshape(2, MROWS, C2)
        acts = [mc[2 * e : 2 * e + 2].reshape(ROWS, C2) for e in range(ENS)]
        network = jnp.dot(
            jnp.concatenate(acts, axis=1), wout[...], preferred_element_type=f32
        )
        parts = []
        for b in range(4):
            t = network[b * C : (b + 1) * C].T
            t = jnp.concatenate([t[0:16], t[16:32]], axis=1)
            high = t.astype(bf16)
            rest = t - high.astype(f32)
            low = rest.astype(bf16)
            parts += [high, low, (rest - low.astype(f32)).astype(bf16)]
        woven = jnp.dot(jnp.concatenate(parts, axis=0), weave, preferred_element_type=f32)
        blocks = [
            woven[b * 48 : b * 48 + 16] + woven[b * 48 + 16 : b * 48 + 32] + woven[b * 48 + 32 : b * 48 + 48]
            for b in range(4)
        ]
        net = jnp.concatenate(blocks, axis=1)
        state = noisy[p].reshape(16, 1024)
        denoised = c_skip * state + c_out * net
        moved = state + (alive(p) * (STEP_RATIO - 1.0)) * (state - denoised)
        out[p] = moved.reshape(ENS, 4, 1024)
        return carry

    lax.fori_loop(0, SLOTS, decode, 0)


def body(
    noisy, sigma, coarse, row_ids, table_index, interp_table, live_counts, face_len, w_lift,
    noise_embed, kernel_top, w_down, kernel_mid, w_up, kernel_dec, w_out,
):
    vmem = pl.BlockSpec(memory_space=pltpu.VMEM)
    smem = pl.BlockSpec(memory_space=pltpu.SMEM)
    units = SLOTS * ENS
    fine = pltpu.VMEM((units, ROWS, C2), bf16)
    mid = pltpu.VMEM((units, MROWS, C2), bf16)
    face = pltpu.VMEM((SLOTS + 1, ENS, 16, C2), bf16)
    faces = pltpu.VMEM((3, SLOTS + 1, ENS, 16, C2), bf16)
    landed = pltpu.VMEM((ENS, 16, C2), bf16)
    return pl.pallas_call(
        kernel,
        out_shape=jax.ShapeDtypeStruct(noisy.shape, f32),
        in_specs=[
            vmem, smem, vmem, vmem, smem, vmem, smem, smem, vmem, vmem,
            vmem, vmem, vmem, vmem, vmem, vmem,
        ],
        out_specs=vmem,
        scratch_shapes=[
            pltpu.VMEM((16, 2048), bf16),
            pltpu.VMEM((1536, C2), bf16),
            pltpu.VMEM((1536, C2), bf16),
            pltpu.VMEM((2304 + C, C2), bf16),
            pltpu.VMEM((C2, C), bf16),
            pltpu.VMEM((ENS * C2, C), bf16),
            pltpu.VMEM((ENS, C2, C2), bf16),
            pltpu.VMEM((2, ROWS, C2), bf16),
            pltpu.VMEM((units, ROWS, C2), f32),
            fine, fine, face, face, face, face,
            pltpu.VMEM((units, MROWS, C), bf16),
            mid, mid, mid, faces, faces,
            landed, landed, landed, landed, landed, landed,
            pltpu.SemaphoreType.DMA((8,)),
            pltpu.SemaphoreType.DMA((8,)),
        ],
        compiler_params=pltpu.CompilerParams(
            collective_id=0, has_side_effects=True, vmem_limit_bytes=63 * 2**20
        ),
        cost_estimate=pl.CostEstimate(
            flops=45_000_000_000, bytes_accessed=6_000_000, transcendentals=15_000_000
        ),
    )(
        noisy, sigma, coarse, row_ids, table_index, interp_table, live_counts, face_len, w_lift,
        noise_embed.reshape(1, C), kernel_top, w_down, kernel_mid, w_up, kernel_dec, w_out,
    )


def solution(mesh):
    placed = (
        P("patch", None, None, None),
        P(),
        P(None, "patch"),
        P("patch", None),
        P("patch"),
        P(),
        P("patch"),
        P("patch", None),
        P(),
        P(),
        P(),
        P(),
        P(),
        P(),
        P(),
        P(),
    )
    return jax.shard_map(
        body, mesh=mesh, in_specs=placed, out_specs=P("patch", None, None, None), check_vma=False
    )
```

```python
import functools

import jax
import jax.numpy as jnp
from jax import lax
from jax.experimental import pallas as pl
from jax.experimental.pallas import tpu as pltpu
from jax.sharding import PartitionSpec as P

MESH = pl.DeviceIdType.MESH
bf16 = jnp.bfloat16
f32 = jnp.float32

SLOTS = 8
ENS = 4
C = 128
C2 = 256
ROWS = 512
MROWS = 256
SIGMA_DATA = 0.5
STEP_RATIO = 0.25
EPSILON = 1e-06

NT = (((1,), (1,)), ((), ()))


def iota(shape, dim):
    return lax.broadcasted_iota(jnp.int32, shape, dim)


def half_rsqrt(x, count):
    total = jnp.sum(x * x, axis=1, keepdims=True)
    return lax.rsqrt(total * (4.0 / count) + 4.0 * EPSILON)


def half_silu(v, scale):
    h = v * scale
    return h + h * jnp.tanh(h)


def act_pair(v):
    halves = []
    for k in range(2):
        x = v[:, k * C : (k + 1) * C]
        scale = half_rsqrt(x, C)
        halves.append(half_silu(x, scale))
    return halves


def act_wide(v):
    scale = half_rsqrt(v, C2)
    return half_silu(v, scale)


def from_left(x):
    x = x.astype(bf16)
    n, c = x.shape
    x3 = x.reshape(n // 16, 16, c)
    return jnp.where(iota(x3.shape, 1) == 0, jnp.zeros((), bf16), pltpu.roll(x3, 1, 1)).reshape(n, c).astype(bf16)


def from_right(x):
    x = x.astype(bf16)
    n, c = x.shape
    x3 = x.reshape(n // 16, 16, c)
    return jnp.where(iota(x3.shape, 1) == 15, jnp.zeros((), bf16), pltpu.roll(x3, 15, 1)).reshape(n, c).astype(bf16)


def transposed(block):
    return block.astype(f32).T.astype(bf16)


def kernel(
    noisy, sigma, coarse, row_ids, table_index, interp, live, face_len, w_lift, embed,
    k_top, w_down, k_mid, w_up, k_dec, w_out,
    out,
    cx, wtop, wdec, wmid, wup, wout, wlift, d_in,
    top, fc, fs, ha, hb, sha, shb, pool, mc, ml, mr, mha, mhb, staged,
    rxa1, rxb1, rxa2, rxb2, rxa3, rxb3, send, recv,
):
    n = lax.axis_size("patch")
    me = lax.axis_index("patch")
    right, left = lax.rem(me + 1, n), lax.rem(me + n - 1, n)
    has_above = jnp.where(me > 0, 1.0, 0.0).astype(f32)
    has_below = jnp.where(me < n - 1, 1.0, 0.0).astype(f32)

    barrier = pltpu.get_barrier_semaphore()
    for neighbour in (left, right):
        pl.semaphore_signal(barrier, inc=1, device_id=(neighbour,), device_id_type=MESH)

    own = jnp.concatenate([coarse[...].astype(f32), jnp.zeros((4, 1024), f32)], axis=0)
    cx[:, 512:1536] = own.astype(bf16)

    def remote(src, dst, k, device):
        return pltpu.make_async_remote_copy(
            src_ref=src, dst_ref=dst, send_sem=send.at[k], recv_sem=recv.at[k],
            device_id=(device,), device_id_type=MESH,
        )

    cells_right = remote(cx.at[:, 1024:1536], cx.at[:, 0:512], 0, right)
    cells_left = remote(cx.at[:, 512:1024], cx.at[:, 1536:2048], 1, left)
    zero = jnp.zeros((C, C), bf16)
    for k_ref, w in ((k_top, wtop), (k_dec, wdec)):

        def fine_weights(dy, carry, k_ref=k_ref, w=w):
            taps = [transposed(k_ref[3 * dy + dx]) for dx in range(3)]
            rows = [(taps[1], taps[0]), (taps[2], taps[1]), (taps[0], zero), (zero, taps[2])]
            for i, (even, odd) in enumerate(rows):
                at = pl.multiple_of(dy * 512 + i * C, C)
                w[pl.ds(at, C), 0:C] = even
                w[pl.ds(at, C), C:C2] = odd
            return carry

        lax.fori_loop(0, 3, fine_weights, 0)

    def mid_weights(t, carry):
        wmid[pl.ds(pl.multiple_of(t * C2, C2), C2), :] = transposed(k_mid[t])
        return carry

    lax.fori_loop(0, 9, mid_weights, 0)
    wmid[2304:, :] = transposed(w_down[...])
    wup[...] = transposed(w_up[...])
    lane = iota((C, C), 0)
    for e in range(ENS):
        for par in range(2):
            z = jnp.zeros((C, C), f32)
            for v in range(4):
                row = w_out[v : v + 1, :].astype(f32)
                z = z + jnp.where(lane == par * 16 + e * 4 + v, row, 0.0)
            wout[e * C2 + par * C : e * C2 + (par + 1) * C, :] = z.T.astype(bf16)
        j = iota((C, 16), 0) % 32
        idx = iota((C, 16), 1)
        pick = ((j // 4 == e) & (idx == j % 4)) | ((j >= 16) & (j < 28) & (idx == j - 12))
        block = jnp.dot(
            jnp.where(pick, 1.0, 0.0).astype(bf16), w_lift[...], preferred_element_type=f32
        )
        b = embed[...] * jnp.log(jnp.full((1, C), sigma[e], f32))
        for k in range(3):
            part = b.astype(bf16).astype(f32)
            block = jnp.where(iota((C, C), 0) % 32 == 28 + k, part, block)
            b = b - part
        block = block.astype(bf16)
        wlift[e, 0:C, 0:C] = block
        wlift[e, 0:C, C:C2] = zero
        wlift[e, C:C2, 0:C] = zero
        wlift[e, C:C2, C:C2] = block

    pl.semaphore_wait(barrier, 2)
    cells_right.start()
    cells_left.start()

    def per_row(f):
        r = iota((16, C), 0) // 4
        s = jnp.full((16, C), sigma[0], f32)
        for e in range(1, ENS):
            s = jnp.where(r == e, sigma[e], s)
        return f(s)[:, 0:1]

    c_in = per_row(lambda s: lax.rsqrt(s * s + SIGMA_DATA * SIGMA_DATA))
    c_skip = per_row(lambda s: SIGMA_DATA * SIGMA_DATA / (s * s + SIGMA_DATA * SIGMA_DATA))
    c_out = per_row(lambda s: s * SIGMA_DATA * lax.rsqrt(s * s + SIGMA_DATA * SIGMA_DATA))

    ids = row_ids[...] - (me * 1024 - 512)
    ids = jnp.concatenate([ids] * 8, axis=1)
    ids = jnp.where(iota((8, C), 1) // 16 == iota((8, C), 0), ids, 0)
    ids = jnp.sum(ids.astype(f32), axis=0, keepdims=True).astype(jnp.int32)
    one_hot = jnp.where(iota((2048, C), 0) == ids, 1.0, 0.0).astype(bf16)
    tab = jnp.zeros((C, C), jnp.int32)
    pk = iota((C, C), 0)
    tk = iota((C, C), 1)
    for p in range(SLOTS):
        tab = jnp.where(pk // 16 == p, table_index[p], tab)
    route = jnp.where((pk % 16 == tk % 16) & (tk // 16 == tab), 1.0, 0.0).astype(bf16)

    cells_right.wait()
    cells_left.wait()
    picked = jnp.dot(cx[...], one_hot, preferred_element_type=f32)
    picked = jnp.concatenate([picked] * 8, axis=0)
    picked = jnp.where(pk // 16 == tk // 16, picked, 0.0).astype(bf16)
    stencil = jnp.dot(picked, route, preferred_element_type=f32).astype(bf16)
    tables = interp[...].reshape(C, 1024)
    cond = jnp.dot(stencil, tables, preferred_element_type=f32)
    cond = jnp.where(iota((C, 1024), 0) % 16 < 12, cond, 1.0).astype(bf16)
    for p in range(SLOTS):
        state = (noisy[p].reshape(16, 1024) * c_in).astype(bf16)
        for b in range(4):
            at = slice(b * C2, (b + 1) * C2)
            mr[b, p * 32 : p * 32 + 16, :] = state[:, at]
            mr[b, p * 32 + 16 : p * 32 + 32, :] = cond[p * 16 : p * 16 + 16, at]

    r = iota((C2, C2), 0)
    cell = iota((C2, C2), 1)
    split = jnp.where(cell == 2 * (r % C) + r // C, 1.0, 0.0).astype(bf16)
    for b in range(4):
        d = lax.dot_general(split, mr[b], NT, preferred_element_type=f32).astype(bf16)
        for t in range(2):
            for par in range(2):
                d_in[t, b * C : (b + 1) * C, par * C : (par + 1) * C] = d[
                    par * C : (par + 1) * C, t * C : (t + 1) * C
                ]

    fine_col = 2 * iota((16, C), 0)
    mid_col = 2 * iota((16, C2), 0)

    def alive(p):
        return jnp.where(jnp.minimum(p, SLOTS - 1 - p) < live[0], 1.0, 0.0).astype(f32)

    def face_of_next(p):
        return jnp.where(p == SLOTS - 1, 32, face_len[0, jnp.minimum(p + 1, SLOTS - 1)])

    def face_of_previous(p):
        return jnp.where(p == 0, 32, face_len[1, jnp.maximum(p - 1, 0)])

    def put_fine_face(centre, side, slot, e, even, odd, length, keep):
        even = jnp.where(fine_col < length, even, 0.0) * keep
        odd = jnp.where(fine_col + 1 < length, odd, 0.0) * keep
        centre[slot, e, :, 0:C] = even.astype(bf16)
        centre[slot, e, :, C:C2] = odd.astype(bf16)
        side[slot, e, :, 0:C] = from_left(odd).astype(bf16)
        side[slot, e, :, C:C2] = from_right(even).astype(bf16)

    def put_fine(p, e, even, odd):
        u = p * ENS + e
        fc[u, :, 0:C] = even.astype(bf16)
        fc[u, :, C:C2] = odd.astype(bf16)
        fs[u, :, 0:C] = from_left(odd).astype(bf16)
        fs[u, :, C:C2] = from_right(even).astype(bf16)
        keep = alive(p)
        put_fine_face(ha, sha, p + 1, e, even[ROWS - 16 :], odd[ROWS - 16 :], face_of_next(p), keep)
        put_fine_face(hb, shb, p, e, even[:16], odd[:16], face_of_previous(p), keep)

    def put_mid_face(faces, slot, e, a, length, keep):
        a = jnp.where(mid_col < length, a, 0.0) * keep
        faces[0, slot, e] = from_left(a).astype(bf16)
        faces[1, slot, e] = a.astype(bf16)
        faces[2, slot, e] = from_right(a).astype(bf16)

    def put_mid(p, e, a):
        u = p * ENS + e
        mc[u] = a.astype(bf16)
        ml[u] = from_left(a).astype(bf16)
        mr[u] = from_right(a).astype(bf16)
        keep = alive(p)
        put_mid_face(mha, p + 1, e, a[MROWS - 16 :], face_of_next(p), keep)
        put_mid_face(mhb, p, e, a[:16], face_of_previous(p), keep)

    def windows(ref, u, above, below, rows):
        return [
            jnp.concatenate([above, ref[u, 0 : rows - 16]], axis=0),
            ref[u],
            jnp.concatenate([ref[u, 16:rows], below], axis=0),
        ]

    def fine_conv(p, e, w):
        u = p * ENS + e
        centre = windows(fc, u, ha[p, e], hb[p + 1, e], ROWS)
        side = windows(fs, u, sha[p, e], shb[p + 1, e], ROWS)
        lhs = jnp.concatenate([x for pair in zip(centre, side) for x in pair], axis=1)
        return jnp.dot(lhs, w[...], preferred_element_type=f32)

    def mid_conv(p, e):
        u = p * ENS + e
        sides = [
            windows(ref, u, mha[k, p, e], mhb[k, p + 1, e], MROWS)
            for k, ref in enumerate((ml, mc, mr))
        ]
        taps = [sides[dx][dy] for dy in range(3) for dx in range(3)]
        lhs = jnp.concatenate(taps + [pool[u]], axis=1)
        return jnp.dot(lhs, wmid[...], preferred_element_type=f32)

    def fine_arrived(rxa, rxb):
        for e in range(ENS):
            a = rxa[e].astype(f32)
            put_fine_face(ha, sha, 0, e, a[:, :C], a[:, C:], face_len[0, 0], has_above)
            b = rxb[e].astype(f32)
            put_fine_face(hb, shb, SLOTS, e, b[:, :C], b[:, C:], face_len[1, SLOTS - 1], has_below)

    def mid_arrived(rxa, rxb):
        for e in range(ENS):
            put_mid_face(mha, 0, e, rxa[e].astype(f32), face_len[0, 0], has_above)
            put_mid_face(mhb, SLOTS, e, rxb[e].astype(f32), face_len[1, SLOTS - 1], has_below)

    def lift(p, e):
        lanes = (iota((1, C2), 1) % C) // 32 == p % 4
        lhs = d_in[p // 4] * jnp.where(lanes, 1.0, 0.0).astype(bf16)
        hidden = jnp.dot(lhs, wlift[e], preferred_element_type=f32)
        top[p * ENS + e] = hidden
        put_fine(p, e, *act_pair(hidden))

    def lift_patch(i, carry):
        for e in range(ENS):
            lift((i + 5) % SLOTS, e)
        return carry

    lax.fori_loop(0, SLOTS - 1, lift_patch, 0)
    face_down = remote(ha.at[SLOTS], rxa1, 2, right)
    face_up = remote(hb.at[0], rxb1, 3, left)
    face_down.start()
    face_up.start()

    def pool_top(p, e):
        u = p * ENS + e
        t = top[u] + fine_conv(p, e, wtop)
        top[u] = t
        pooled = (t[:, :C] + t[:, C:]).reshape(16, 2, 16, C)
        pooled = ((pooled[:, 0] + pooled[:, 1]) * 0.25).reshape(MROWS, C).astype(bf16)
        pool[u] = pooled
        staged[e, :, 0:C] = pooled

    def project(p, e):
        d = jnp.dot(staged[e, :, 0:C], wmid[2304:, :], preferred_element_type=f32)
        put_mid(p, e, act_wide(d))

    def encode(i, carry):
        @pl.when(i == 5)
        def _():
            face_down.wait()
            face_up.wait()
            fine_arrived(rxa1, rxb1)

        for e in range(ENS):
            project((i + 1) % SLOTS, e)
            pool_top((i + 2) % SLOTS, e)
        return carry

    for e in range(ENS):
        lift(4, e)
        pool_top(2, e)
    lax.fori_loop(1, SLOTS, encode, 0)
    mid_down = remote(mha.at[1, SLOTS], rxa2, 4, right)
    mid_up = remote(mhb.at[1, 0], rxb2, 5, left)
    mid_down.start()
    mid_up.start()

    def mix(p, e):
        staged[e] = mid_conv(p, e).astype(bf16)

    def merge(p, e):
        u = p * ENS + e
        up = jnp.dot(staged[e], wup[...], preferred_element_type=f32).reshape(16, 1, 16, C)
        up = jnp.broadcast_to(up, (16, 2, 16, C)).reshape(ROWS, C)
        merged = top[u] + jnp.concatenate([up, up], axis=1)
        top[u] = merged
        put_fine(p, e, *act_pair(merged))

    def middle(i, carry):
        @pl.when(i == 4)
        def _():
            mid_down.wait()
            mid_up.wait()
            mid_arrived(rxa2, rxb2)

        for e in range(ENS):
            merge((i + 2) % SLOTS, e)
            mix((i + 3) % SLOTS, e)
        return carry

    for e in range(ENS):
        project(1, e)
        mix(3, e)
    lax.fori_loop(1, SLOTS, middle, 0)
    last_down = remote(ha.at[SLOTS], rxa3, 6, right)
    last_up = remote(hb.at[0], rxb3, 7, left)
    last_down.start()
    last_up.start()

    cell_col = iota((C2, C2), 1)
    src = iota((C2, C2), 0)
    weave = jnp.where(cell_col == 2 * (src % C) + src // C, 1.0, 0.0).astype(bf16)

    def unfold(p, e):
        even, odd = act_pair(top[p * ENS + e] + fine_conv(p, e, wdec))
        acts = jnp.concatenate([even, odd], axis=1).astype(bf16)
        mc[2 * e : 2 * e + 2] = acts.reshape(2, MROWS, C2)

    def finish(p):
        acts = [mc[2 * e : 2 * e + 2].reshape(ROWS, C2) for e in range(ENS)]
        network = jnp.dot(
            jnp.concatenate(acts, axis=1), wout[...], preferred_element_type=f32
        )
        parts = []
        for b in range(4):
            t = network[b * C : (b + 1) * C].T
            t = jnp.concatenate([t[0:16], t[16:32]], axis=1)
            high = t.astype(bf16)
            rest = t - high.astype(f32)
            low = rest.astype(bf16)
            parts += [high, low, (rest - low.astype(f32)).astype(bf16)]
        woven = jnp.dot(jnp.concatenate(parts, axis=0), weave, preferred_element_type=f32)
        blocks = [
            woven[b * 48 : b * 48 + 16] + woven[b * 48 + 16 : b * 48 + 32] + woven[b * 48 + 32 : b * 48 + 48]
            for b in range(4)
        ]
        net = jnp.concatenate(blocks, axis=1)
        state = noisy[p].reshape(16, 1024)
        denoised = c_skip * state + c_out * net
        moved = state + (alive(p) * (STEP_RATIO - 1.0)) * (state - denoised)
        out[p] = moved.reshape(ENS, 4, 1024)

    def decode(i, carry):
        @pl.when(i == 3)
        def _():
            last_down.wait()
            last_up.wait()
            fine_arrived(rxa3, rxb3)

        for e in range(ENS):
            unfold((i + 4) % SLOTS, e)
        finish((i + 4) % SLOTS)
        return carry

    for e in range(ENS):
        merge(2, e)
        unfold(4, e)
    finish(4)
    lax.fori_loop(1, SLOTS, decode, 0)


def body(
    noisy, sigma, coarse, row_ids, table_index, interp_table, live_counts, face_len, w_lift,
    noise_embed, kernel_top, w_down, kernel_mid, w_up, kernel_dec, w_out,
):
    vmem = pl.BlockSpec(memory_space=pltpu.VMEM)
    smem = pl.BlockSpec(memory_space=pltpu.SMEM)
    units = SLOTS * ENS
    fine = pltpu.VMEM((units, ROWS, C2), bf16)
    mid = pltpu.VMEM((units, MROWS, C2), bf16)
    face = pltpu.VMEM((SLOTS + 1, ENS, 16, C2), bf16)
    faces = pltpu.VMEM((3, SLOTS + 1, ENS, 16, C2), bf16)
    landed = pltpu.VMEM((ENS, 16, C2), bf16)
    return pl.pallas_call(
        kernel,
        out_shape=jax.ShapeDtypeStruct(noisy.shape, f32),
        in_specs=[
            vmem, smem, vmem, vmem, smem, vmem, smem, smem, vmem, vmem,
            vmem, vmem, vmem, vmem, vmem, vmem,
        ],
        out_specs=vmem,
        scratch_shapes=[
            pltpu.VMEM((16, 2048), bf16),
            pltpu.VMEM((1536, C2), bf16),
            pltpu.VMEM((1536, C2), bf16),
            pltpu.VMEM((2304 + C, C2), bf16),
            pltpu.VMEM((C2, C), bf16),
            pltpu.VMEM((ENS * C2, C), bf16),
            pltpu.VMEM((ENS, C2, C2), bf16),
            pltpu.VMEM((2, ROWS, C2), bf16),
            pltpu.VMEM((units, ROWS, C2), f32),
            fine, fine, face, face, face, face,
            pltpu.VMEM((units, MROWS, C), bf16),
            mid, mid, mid, faces, faces, pltpu.VMEM((ENS, MROWS, C2), bf16),
            landed, landed, landed, landed, landed, landed,
            pltpu.SemaphoreType.DMA((8,)),
            pltpu.SemaphoreType.DMA((8,)),
        ],
        compiler_params=pltpu.CompilerParams(
            collective_id=0, has_side_effects=True, vmem_limit_bytes=63 * 2**20
        ),
        cost_estimate=pl.CostEstimate(
            flops=45_000_000_000, bytes_accessed=6_000_000, transcendentals=15_000_000
        ),
    )(
        noisy, sigma, coarse, row_ids, table_index, interp_table, live_counts, face_len.T, w_lift.T,
        noise_embed.reshape(1, C), kernel_top, w_down, kernel_mid, w_up, kernel_dec, w_out,
    )


def solution(mesh):
    placed = (
        P("patch", None, None, None),
        P(),
        P(None, "patch"),
        P("patch", None),
        P("patch"),
        P(),
        P("patch"),
        P("patch", None),
        P(),
        P(),
        P(),
        P(),
        P(),
        P(),
        P(),
        P(),
    )
    return jax.shard_map(
        body, mesh=mesh, in_specs=placed, out_specs=P("patch", None, None, None), check_vma=False
    )
```

```python
import functools

import jax
import jax.numpy as jnp
from jax import lax
from jax.experimental import pallas as pl
from jax.experimental.pallas import tpu as pltpu
from jax.sharding import PartitionSpec as P

MESH = pl.DeviceIdType.MESH
bf16 = jnp.bfloat16
f32 = jnp.float32

SLOTS = 8
ENS = 4
C = 128
C2 = 256
ROWS = 512
MROWS = 256
SIGMA_DATA = 0.5
STEP_RATIO = 0.25
EPSILON = 1e-06

NT = (((1,), (1,)), ((), ()))


def iota(shape, dim):
    return lax.broadcasted_iota(jnp.int32, shape, dim)


def half_rsqrt(x, count):
    total = jnp.sum(x * x, axis=1, keepdims=True)
    return lax.rsqrt(total * (4.0 / count) + 4.0 * EPSILON)


def half_silu(v, scale):
    h = v * scale
    return h + h * jnp.tanh(h)


def act_pair(v):
    halves = []
    for k in range(2):
        x = v[:, k * C : (k + 1) * C]
        scale = half_rsqrt(x, C)
        halves.append(half_silu(x, scale))
    return halves


def act_wide(v):
    scale = half_rsqrt(v, C2)
    return half_silu(v, scale)


def from_left(x):
    n, c = x.shape
    r = pltpu.roll(x.reshape(n // 8, 8, c), 1, 1).reshape(n // 16, 2, 8, c)
    edge = iota((n // 16, 8, c), 1) == 0
    low = jnp.where(edge, 0.0, r[:, 0])
    high = jnp.where(edge, r[:, 0], r[:, 1])
    return jnp.stack([low, high], axis=1).reshape(n, c)


def from_right(x):
    n, c = x.shape
    r = pltpu.roll(x.reshape(n // 8, 8, c), 7, 1).reshape(n // 16, 2, 8, c)
    edge = iota((n // 16, 8, c), 1) == 7
    low = jnp.where(edge, r[:, 1], r[:, 0])
    high = jnp.where(edge, 0.0, r[:, 1])
    return jnp.stack([low, high], axis=1).reshape(n, c)


def transposed(block):
    return block.astype(f32).T.astype(bf16)


def kernel(
    noisy, sigma, coarse, row_ids, table_index, interp, live, face_len, w_lift, embed,
    k_top, w_down, k_mid, w_up, k_dec, w_out,
    out,
    cx, wtop, wdec, wmid, wup, wout, wlift, d_in,
    top, fc, fs, ha, hb, sha, shb, pool, mc, ml, mr, mha, mhb, staged,
    txa, txb, rxa1, rxb1, rxa2, rxb2, rxa3, rxb3, send, recv,
):
    n = lax.axis_size("patch")
    me = lax.axis_index("patch")
    right, left = lax.rem(me + 1, n), lax.rem(me + n - 1, n)
    has_above = jnp.where(me > 0, 1.0, 0.0).astype(f32)
    has_below = jnp.where(me < n - 1, 1.0, 0.0).astype(f32)

    barrier = pltpu.get_barrier_semaphore()
    for neighbour in (left, right):
        pl.semaphore_signal(barrier, inc=1, device_id=(neighbour,), device_id_type=MESH)

    own = jnp.concatenate([coarse[...].astype(f32), jnp.zeros((4, 1024), f32)], axis=0)
    cx[:, 512:1536] = own.astype(bf16)

    def remote(src, dst, k, device):
        return pltpu.make_async_remote_copy(
            src_ref=src, dst_ref=dst, send_sem=send.at[k], recv_sem=recv.at[k],
            device_id=(device,), device_id_type=MESH,
        )

    cells_right = remote(cx.at[:, 1024:1536], cx.at[:, 0:512], 0, right)
    cells_left = remote(cx.at[:, 512:1024], cx.at[:, 1536:2048], 1, left)
    zero = jnp.zeros((C, C), bf16)
    for k_ref, w in ((k_top, wtop), (k_dec, wdec)):

        def fine_weights(dy, carry, k_ref=k_ref, w=w):
            taps = [transposed(k_ref[3 * dy + dx]) for dx in range(3)]
            rows = [(taps[1], taps[0]), (taps[2], taps[1]), (taps[0], zero), (zero, taps[2])]
            for i, (even, odd) in enumerate(rows):
                at = pl.multiple_of(dy * 512 + i * C, C)
                w[pl.ds(at, C), 0:C] = even
                w[pl.ds(at, C), C:C2] = odd
            return carry

        lax.fori_loop(0, 3, fine_weights, 0)

    pl.semaphore_wait(barrier, 2)
    cells_right.start()
    cells_left.start()

    def mid_weights(t, carry):
        wmid[pl.ds(pl.multiple_of(t * C2, C2), C2), :] = transposed(k_mid[t])
        return carry

    lax.fori_loop(0, 9, mid_weights, 0)
    wmid[2304:, :] = transposed(w_down[...])
    wup[...] = transposed(w_up[...])
    lane = iota((C, C), 0)
    for e in range(ENS):
        for par in range(2):
            z = jnp.zeros((C, C), f32)
            for v in range(4):
                row = w_out[v : v + 1, :].astype(f32)
                z = z + jnp.where(lane == par * 16 + e * 4 + v, row, 0.0)
            wout[e * C2 + par * C : e * C2 + (par + 1) * C, :] = z.T.astype(bf16)
        j = iota((C, 16), 0) % 32
        idx = iota((C, 16), 1)
        pick = ((j // 4 == e) & (idx == j % 4)) | ((j >= 16) & (j < 28) & (idx == j - 12))
        block = jnp.dot(
            jnp.where(pick, 1.0, 0.0).astype(bf16), w_lift[...], preferred_element_type=f32
        )
        b = embed[...] * jnp.log(jnp.full((1, C), sigma[e], f32))
        for k in range(3):
            part = b.astype(bf16).astype(f32)
            block = jnp.where(iota((C, C), 0) % 32 == 28 + k, part, block)
            b = b - part
        block = block.astype(bf16)
        wlift[e, 0:C, 0:C] = block
        wlift[e, 0:C, C:C2] = zero
        wlift[e, C:C2, 0:C] = zero
        wlift[e, C:C2, C:C2] = block

    def per_row(f):
        r = iota((16, C), 0) // 4
        s = jnp.full((16, C), sigma[0], f32)
        for e in range(1, ENS):
            s = jnp.where(r == e, sigma[e], s)
        return f(s)[:, 0:1]

    c_in = per_row(lambda s: lax.rsqrt(s * s + SIGMA_DATA * SIGMA_DATA))
    c_skip = per_row(lambda s: SIGMA_DATA * SIGMA_DATA / (s * s + SIGMA_DATA * SIGMA_DATA))
    c_out = per_row(lambda s: s * SIGMA_DATA * lax.rsqrt(s * s + SIGMA_DATA * SIGMA_DATA))

    ids = row_ids[...] - (me * 1024 - 512)
    ids = jnp.concatenate([ids] * 8, axis=1)
    ids = jnp.where(iota((8, C), 1) // 16 == iota((8, C), 0), ids, 0)
    ids = jnp.sum(ids.astype(f32), axis=0, keepdims=True).astype(jnp.int32)
    one_hot = jnp.where(iota((2048, C), 0) == ids, 1.0, 0.0).astype(bf16)
    tab = jnp.zeros((C, C), jnp.int32)
    pk = iota((C, C), 0)
    tk = iota((C, C), 1)
    for p in range(SLOTS):
        tab = jnp.where(pk // 16 == p, table_index[p], tab)
    route = jnp.where((pk % 16 == tk % 16) & (tk // 16 == tab), 1.0, 0.0).astype(bf16)

    cells_right.wait()
    cells_left.wait()
    picked = jnp.dot(cx[...], one_hot, preferred_element_type=f32)
    picked = jnp.concatenate([picked] * 8, axis=0)
    picked = jnp.where(pk // 16 == tk // 16, picked, 0.0).astype(bf16)
    stencil = jnp.dot(picked, route, preferred_element_type=f32).astype(bf16)
    tables = interp[...].reshape(C, 1024)
    cond = jnp.dot(stencil, tables, preferred_element_type=f32)
    cond = jnp.where(iota((C, 1024), 0) % 16 < 12, cond, 1.0).astype(bf16)
    for p in range(SLOTS):
        state = (noisy[p].reshape(16, 1024) * c_in).astype(bf16)
        for b in range(4):
            at = slice(b * C2, (b + 1) * C2)
            mr[b, p * 32 : p * 32 + 16, :] = state[:, at]
            mr[b, p * 32 + 16 : p * 32 + 32, :] = cond[p * 16 : p * 16 + 16, at]

    r = iota((C2, C2), 0)
    cell = iota((C2, C2), 1)
    split = jnp.where(cell == 2 * (r % C) + r // C, 1.0, 0.0).astype(bf16)
    for b in range(4):
        d = lax.dot_general(split, mr[b], NT, preferred_element_type=f32).astype(bf16)
        for t in range(2):
            for par in range(2):
                d_in[t, b * C : (b + 1) * C, par * C : (par + 1) * C] = d[
                    par * C : (par + 1) * C, t * C : (t + 1) * C
                ]

    fine_col = 2 * iota((16, C), 0)
    mid_col = 2 * iota((16, C2), 0)

    def alive(p):
        return jnp.where(jnp.minimum(p, SLOTS - 1 - p) < live[0], 1.0, 0.0).astype(f32)

    def face_of_next(p):
        return jnp.where(p == SLOTS - 1, 32, face_len[0, jnp.minimum(p + 1, SLOTS - 1)])

    def face_of_previous(p):
        return jnp.where(p == 0, 32, face_len[1, jnp.maximum(p - 1, 0)])

    def put_fine_face(centre, side, slot, e, even, odd, length, keep):
        even = jnp.where(fine_col < length, even, 0.0) * keep
        odd = jnp.where(fine_col + 1 < length, odd, 0.0) * keep
        centre[slot, e, :, 0:C] = even.astype(bf16)
        centre[slot, e, :, C:C2] = odd.astype(bf16)
        side[slot, e, :, 0:C] = from_left(odd).astype(bf16)
        side[slot, e, :, C:C2] = from_right(even).astype(bf16)

    def put_fine(p, e, even, odd):
        u = p * ENS + e
        fc[u, :, 0:C] = even.astype(bf16)
        fc[u, :, C:C2] = odd.astype(bf16)
        fs[u, :, 0:C] = from_left(odd).astype(bf16)
        fs[u, :, C:C2] = from_right(even).astype(bf16)
        keep = alive(p)
        put_fine_face(ha, sha, p + 1, e, even[ROWS - 16 :], odd[ROWS - 16 :], face_of_next(p), keep)
        put_fine_face(hb, shb, p, e, even[:16], odd[:16], face_of_previous(p), keep)

    def put_mid_face(faces, slot, e, a, length, keep):
        a = jnp.where(mid_col < length, a, 0.0) * keep
        faces[0, slot, e] = from_left(a).astype(bf16)
        faces[1, slot, e] = a.astype(bf16)
        faces[2, slot, e] = from_right(a).astype(bf16)

    def put_mid(p, e, a):
        u = p * ENS + e
        mc[u] = a.astype(bf16)
        ml[u] = from_left(a).astype(bf16)
        mr[u] = from_right(a).astype(bf16)
        keep = alive(p)
        put_mid_face(mha, p + 1, e, a[MROWS - 16 :], face_of_next(p), keep)
        put_mid_face(mhb, p, e, a[:16], face_of_previous(p), keep)

    def windows(ref, u, above, below, rows):
        return [
            jnp.concatenate([above, ref[u, 0 : rows - 16]], axis=0),
            ref[u],
            jnp.concatenate([ref[u, 16:rows], below], axis=0),
        ]

    def fine_conv(p, e, w):
        u = p * ENS + e
        centre = windows(fc, u, ha[p, e], hb[p + 1, e], ROWS)
        side = windows(fs, u, sha[p, e], shb[p + 1, e], ROWS)
        lhs = jnp.concatenate([x for pair in zip(centre, side) for x in pair], axis=1)
        return jnp.dot(lhs, w[...], preferred_element_type=f32)

    def mid_conv(p, e):
        u = p * ENS + e
        sides = [
            windows(ref, u, mha[k, p, e], mhb[k, p + 1, e], MROWS)
            for k, ref in enumerate((ml, mc, mr))
        ]
        taps = [sides[dx][dy] for dy in range(3) for dx in range(3)]
        lhs = jnp.concatenate(taps + [pool[u]], axis=1)
        return jnp.dot(lhs, wmid[...], preferred_element_type=f32)

    def fine_arrived(rxa, rxb):
        for e in range(ENS):
            a = rxa[e].astype(f32)
            put_fine_face(ha, sha, 0, e, a[:, :C], a[:, C:], face_len[0, 0], has_above)
            b = rxb[e].astype(f32)
            put_fine_face(hb, shb, SLOTS, e, b[:, :C], b[:, C:], face_len[1, SLOTS - 1], has_below)

    def mid_arrived(rxa, rxb):
        for e in range(ENS):
            put_mid_face(mha, 0, e, rxa[e].astype(f32), face_len[0, 0], has_above)
            put_mid_face(mhb, SLOTS, e, rxb[e].astype(f32), face_len[1, SLOTS - 1], has_below)

    def lift(p, e):
        lanes = (iota((1, C2), 1) % C) // 32 == p % 4
        lhs = d_in[p // 4] * jnp.where(lanes, 1.0, 0.0).astype(bf16)
        hidden = jnp.dot(lhs, wlift[e], preferred_element_type=f32)
        top[p * ENS + e] = hidden
        put_fine(p, e, *act_pair(hidden))

    def edge(p, e, at, target):
        lanes = (iota((1, C2), 1) % C) // 32 == p % 4
        lhs = d_in[p // 4, at : at + 16] * jnp.where(lanes, 1.0, 0.0).astype(bf16)
        hidden = jnp.dot(lhs, wlift[e], preferred_element_type=f32)
        target[e] = jnp.concatenate(act_pair(hidden), axis=1).astype(bf16)

    for e in range(ENS):
        edge(SLOTS - 1, e, ROWS - 16, txa)
        edge(0, e, 0, txb)
    face_down = remote(txa, rxa1, 2, right)
    face_up = remote(txb, rxb1, 3, left)
    face_down.start()
    face_up.start()

    def lift_patch(p, carry):
        for e in range(ENS):
            lift(p, e)
        return carry

    lax.fori_loop(1, 4, lift_patch, 0)

    def pool_top(p, e):
        u = p * ENS + e
        t = top[u] + fine_conv(p, e, wtop)
        top[u] = t
        pooled = (t[:, :C] + t[:, C:]).reshape(16, 2, 16, C)
        pooled = ((pooled[:, 0] + pooled[:, 1]) * 0.25).reshape(MROWS, C).astype(bf16)
        pool[u] = pooled
        staged[e, :, 0:C] = pooled

    def project(p, e):
        d = jnp.dot(staged[e, :, 0:C], wmid[2304:, :], preferred_element_type=f32)
        put_mid(p, e, act_wide(d))

    def encode_lift(i, carry):
        for e in range(ENS):
            project((i + 1) % SLOTS, e)
            pool_top((i + 2) % SLOTS, e)
        for e in range(ENS):
            lift((i + 4) % SLOTS, e)
        return carry

    def encode(i, carry):
        for e in range(ENS):
            project((i + 1) % SLOTS, e)
            pool_top((i + 2) % SLOTS, e)
        return carry

    for e in range(ENS):
        lift(4, e)
        pool_top(2, e)
    lax.fori_loop(1, 5, encode_lift, 0)
    face_down.wait()
    face_up.wait()
    fine_arrived(rxa1, rxb1)
    lax.fori_loop(5, SLOTS, encode, 0)
    mid_down = remote(mha.at[1, SLOTS], rxa2, 4, right)
    mid_up = remote(mhb.at[1, 0], rxb2, 5, left)
    mid_down.start()
    mid_up.start()

    def mix(p, e):
        staged[e] = mid_conv(p, e).astype(bf16)

    def merge(p, e):
        u = p * ENS + e
        up = jnp.dot(staged[e], wup[...], preferred_element_type=f32).reshape(16, 1, 16, C)
        up = jnp.broadcast_to(up, (16, 2, 16, C)).reshape(ROWS, C)
        merged = top[u] + jnp.concatenate([up, up], axis=1)
        top[u] = merged
        put_fine(p, e, *act_pair(merged))

    def middle(i, carry):
        @pl.when(i == 4)
        def _():
            mid_down.wait()
            mid_up.wait()
            mid_arrived(rxa2, rxb2)

        for e in range(ENS):
            merge((i + 2) % SLOTS, e)
            mix((i + 3) % SLOTS, e)
        return carry

    for e in range(ENS):
        project(1, e)
        mix(3, e)
    lax.fori_loop(1, SLOTS, middle, 0)
    last_down = remote(ha.at[SLOTS], rxa3, 6, right)
    last_up = remote(hb.at[0], rxb3, 7, left)
    last_down.start()
    last_up.start()

    cell_col = iota((C2, C2), 1)
    src = iota((C2, C2), 0)
    weave = jnp.where(cell_col == 2 * (src % C) + src // C, 1.0, 0.0).astype(bf16)

    def unfold(p, e):
        even, odd = act_pair(top[p * ENS + e] + fine_conv(p, e, wdec))
        acts = jnp.concatenate([even, odd], axis=1).astype(bf16)
        mc[2 * e : 2 * e + 2] = acts.reshape(2, MROWS, C2)

    def finish(p):
        acts = [mc[2 * e : 2 * e + 2].reshape(ROWS, C2) for e in range(ENS)]
        network = jnp.dot(
            jnp.concatenate(acts, axis=1), wout[...], preferred_element_type=f32
        )
        parts = []
        for b in range(4):
            t = network[b * C : (b + 1) * C].T
            t = jnp.concatenate([t[0:16], t[16:32]], axis=1)
            high = t.astype(bf16)
            rest = t - high.astype(f32)
            low = rest.astype(bf16)
            parts += [high, low, (rest - low.astype(f32)).astype(bf16)]
        woven = jnp.dot(jnp.concatenate(parts, axis=0), weave, preferred_element_type=f32)
        blocks = [
            woven[b * 48 : b * 48 + 16] + woven[b * 48 + 16 : b * 48 + 32] + woven[b * 48 + 32 : b * 48 + 48]
            for b in range(4)
        ]
        net = jnp.concatenate(blocks, axis=1)
        state = noisy[p].reshape(16, 1024)
        denoised = c_skip * state + c_out * net
        moved = state + (alive(p) * (STEP_RATIO - 1.0)) * (state - denoised)
        out[p] = moved.reshape(ENS, 4, 1024)

    def decode(i, carry):
        @pl.when(i == 3)
        def _():
            last_down.wait()
            last_up.wait()
            fine_arrived(rxa3, rxb3)

        for e in range(ENS):
            unfold((i + 4) % SLOTS, e)
        finish((i + 4) % SLOTS)
        return carry

    for e in range(ENS):
        merge(2, e)
        unfold(4, e)
    finish(4)
    lax.fori_loop(1, SLOTS, decode, 0)


def body(
    noisy, sigma, coarse, row_ids, table_index, interp_table, live_counts, face_len, w_lift,
    noise_embed, kernel_top, w_down, kernel_mid, w_up, kernel_dec, w_out,
):
    vmem = pl.BlockSpec(memory_space=pltpu.VMEM)
    smem = pl.BlockSpec(memory_space=pltpu.SMEM)
    units = SLOTS * ENS
    fine = pltpu.VMEM((units, ROWS, C2), bf16)
    mid = pltpu.VMEM((units, MROWS, C2), bf16)
    face = pltpu.VMEM((SLOTS + 1, ENS, 16, C2), bf16)
    faces = pltpu.VMEM((3, SLOTS + 1, ENS, 16, C2), bf16)
    landed = pltpu.VMEM((ENS, 16, C2), bf16)
    return pl.pallas_call(
        kernel,
        out_shape=jax.ShapeDtypeStruct(noisy.shape, f32),
        in_specs=[
            vmem, smem, vmem, vmem, smem, vmem, smem, smem, vmem, vmem,
            vmem, vmem, vmem, vmem, vmem, vmem,
        ],
        out_specs=vmem,
        scratch_shapes=[
            pltpu.VMEM((16, 2048), bf16),
            pltpu.VMEM((1536, C2), bf16),
            pltpu.VMEM((1536, C2), bf16),
            pltpu.VMEM((2304 + C, C2), bf16),
            pltpu.VMEM((C2, C), bf16),
            pltpu.VMEM((ENS * C2, C), bf16),
            pltpu.VMEM((ENS, C2, C2), bf16),
            pltpu.VMEM((2, ROWS, C2), bf16),
            pltpu.VMEM((units, ROWS, C2), f32),
            fine, fine, face, face, face, face,
            pltpu.VMEM((units, MROWS, C), bf16),
            mid, mid, mid, faces, faces, pltpu.VMEM((ENS, MROWS, C2), bf16),
            landed, landed, landed, landed, landed, landed, landed, landed,
            pltpu.SemaphoreType.DMA((8,)),
            pltpu.SemaphoreType.DMA((8,)),
        ],
        compiler_params=pltpu.CompilerParams(
            collective_id=0, has_side_effects=True, vmem_limit_bytes=63 * 2**20
        ),
        cost_estimate=pl.CostEstimate(
            flops=45_000_000_000, bytes_accessed=6_000_000, transcendentals=15_000_000
        ),
    )(
        noisy, sigma, coarse, row_ids, table_index, interp_table, live_counts, face_len.T, w_lift.T,
        noise_embed.reshape(1, C), kernel_top, w_down, kernel_mid, w_up, kernel_dec, w_out,
    )


def solution(mesh):
    placed = (
        P("patch", None, None, None),
        P(),
        P(None, "patch"),
        P("patch", None),
        P("patch"),
        P(),
        P("patch"),
        P("patch", None),
        P(),
        P(),
        P(),
        P(),
        P(),
        P(),
        P(),
        P(),
    )
    return jax.shard_map(
        body, mesh=mesh, in_specs=placed, out_specs=P("patch", None, None, None), check_vma=False
    )
```
